32 devices in a mesh: groups: 2 (over y), dp: 4 (over x, core), tensor: 4 (over z).
Axes of the slice: x: 2, y: 2, z: 4, core: 2. Of those that a mesh axis runs over, the one named last changes fastest.
Arguments:
- hidden: bfloat16 [512, 8192], P(('groups', 'dp', 'tensor')), parts along dimension 0, may hold values from -6 to 6
- query_weight: bfloat16 [8192, 4096], P(None, 'tensor'), may hold values from -0.0625 to 0.0625
- adapter_shrink: bfloat16 [64, 8192, 64], P('dp', 'tensor'), may hold values from -0.0625 to 0.0625
- adapter_expand: bfloat16 [64, 64, 4096], P('dp', None, 'tensor'), may hold values from -0.75 to 0.75
- adapter_page_table: int32 [128], P('groups'), parts along dimension 0, may hold values from 0 to 63, as said below
- request_adapter_index: int32 [512], P(('groups', 'dp', 'tensor')), parts along dimension 0, may hold values from 0 to 63, as said below
- key_value_cache: bfloat16 [512, 128, 2, 512], P(('groups', 'dp', 'tensor')), parts along dimension 0, may hold values from -800 to 800
- cached_lengths: int32 [512], P(('groups', 'dp', 'tensor')), parts along dimension 0, may hold values from 16 to 128, as said below
Outputs:
- attended: bfloat16 [512, 4096], P(('groups', 'dp', 'tensor')), parts along dimension 0
The draws below stay inside these ranges and needn't reach their ends.
There are 2 independent parts, one for each index of `groups`. The reference program is written for one: setup_inputs(seed, part) draws one part's arguments, and reference() takes and returns one part's arrays. A program takes and returns all parts, laid end to end along the dimension named above; an argument that names none is the same for every part. Nothing has to cross between parts.
Inputs may be any that keep to these rules, and one draw needn't show every extreme that they name: `adapter_page_table`: each replica's table is a permutation of the 64 pages; page p lies on dp index p // 16. `request_adapter_index`: among the 64 requests of one dp index, at most 24 use adapters whose pages lie on one dp index; in every replica one dp index's pages serve exactly 24 requests of every dp index. `cached_lengths`: some request of every replica has exactly 128 cached positions.
All inputs are finite; a program needn't handle non-finite values.
Results may differ from the reference program's by a relative error of at most 0.012.
The reference program's roundings to bfloat16 on the way count: a program that leaves them out, or rounds other values in their place, can miss the bound.
Values may be sent and summed in bfloat16 or wider, within the bound.
A program may use at most 128 MiB of HBM per device.

```python
import math
import jax
import jax.numpy as jnp
from jax import lax

MODEL_WIDTH = 8192
QUERY_HEADS = 32
KVH = 4
HEAD_SIZE = 128
ADAPTER_RANK = 64
PAGE_DEV = 16
CACHE = 128
REQS = 256
ROW_REQS = 64
ADAPTER_PAGES = 64
CAP = 24


def pages_and_requests(key):
    page_order = jax.random.permutation(jax.random.fold_in(key, 11), ADAPTER_PAGES).astype(jnp.int32)
    inverse = jnp.zeros((ADAPTER_PAGES,), jnp.int32).at[page_order].set(jnp.arange(ADAPTER_PAGES, dtype=jnp.int32))
    owners = ADAPTER_PAGES // PAGE_DEV
    slots = owners * CAP
    row_groups = REQS // ROW_REQS
    forced = jax.random.randint(jax.random.fold_in(key, 12), (), 0, owners)
    row_keys = jax.random.split(jax.random.fold_in(key, 13), row_groups)

    def one_row(row_key):
        first_key, second_key, third_key = jax.random.split(row_key, 3)
        scores = jax.random.permutation(first_key, slots).astype(jnp.int32)
        scores = jnp.where(jnp.arange(slots, dtype=jnp.int32) // CAP == forced, scores - slots, scores)
        ranking = jnp.argsort(scores)
        selected_pages = ranking[:ROW_REQS]
        selected_pages = selected_pages[jax.random.permutation(second_key, ROW_REQS)]
        owner_index = (selected_pages // CAP).astype(jnp.int32)
        return owner_index * PAGE_DEV + jax.random.randint(third_key, (ROW_REQS,), 0, PAGE_DEV)
    page_slots = jax.vmap(one_row)(row_keys).reshape(REQS)
    return (page_order, inverse[page_slots].astype(jnp.int32))


def draw_adapter_page_table(key, part):
    return pages_and_requests(key)[0]


def draw_request_adapter_index(key, part):
    return pages_and_requests(key)[1]


def draw_cached_lengths(key, part):
    key = jax.random.fold_in(key, 21)
    lengths = jax.random.randint(key, (REQS,), CACHE // 8, CACHE + 1)
    return lengths.at[0].set(CACHE).astype(jnp.int32)


def draw_key_value_cache(key, part):
    key = jax.random.fold_in(key, 31)
    first_key = jax.random.fold_in(key, 0)
    background = jnp.clip(jax.random.normal(first_key, (REQS, CACHE, 2, KVH * HEAD_SIZE), jnp.float32), -6.0, 6.0)
    return background.astype(jnp.bfloat16)


def block_levels(key, extent, cuts, least, high):
    def one(position, blocks):
        steps = jax.random.uniform(jax.random.fold_in(jax.random.fold_in(key, 6), position), (blocks,), jnp.float32, least / len(cuts), high / len(cuts))
        return jnp.repeat(jnp.exp(steps), extent[position] // blocks).reshape((-1,) + (1,) * (len(extent) - position - 1))

    level = one(*cuts[0])
    for cut in cuts[1:]:
        level = level * one(*cut)
    return level


def bell_draw(rng, extent, deviation, bound, cuts=(), kind=jnp.bfloat16):
    entries = deviation * jax.random.normal(rng, extent, jnp.float32)
    if cuts:
        entries = entries * block_levels(rng, extent, cuts, -0.22, 0.18)
    return jnp.clip(entries, -bound, bound).astype(kind)


def setup_inputs(seed: int = 0, part: int = 0) -> dict:
    seeds = jax.random.split(jax.random.key(seed), 9)
    part_keys = jax.random.split(jax.random.fold_in(seeds[8], part), 9)
    hidden = bell_draw(part_keys[0], (REQS, MODEL_WIDTH), 1.0, 6.0, ((0, 16),))
    query_weight = bell_draw(seeds[1], (MODEL_WIDTH, QUERY_HEADS * HEAD_SIZE), MODEL_WIDTH ** -0.5, 0.0625, ((1, 4),))
    adapter_shrink = bell_draw(seeds[2], (ADAPTER_PAGES, MODEL_WIDTH, ADAPTER_RANK), MODEL_WIDTH ** -0.5, 0.0625, ((0, 4), (1, 4)))
    adapter_expand = bell_draw(seeds[3], (ADAPTER_PAGES, ADAPTER_RANK, QUERY_HEADS * HEAD_SIZE), ADAPTER_RANK ** -0.5, 0.75, ((0, 4), (2, 4)))
    adapter_page_table = draw_adapter_page_table(jax.random.fold_in(jax.random.fold_in(seeds[8], part), 71), part)
    request_adapter_index = draw_request_adapter_index(jax.random.fold_in(jax.random.fold_in(seeds[8], part), 71), part)
    key_value_cache = draw_key_value_cache(jax.random.fold_in(jax.random.fold_in(seeds[8], part), 71), part)
    cached_lengths = draw_cached_lengths(jax.random.fold_in(jax.random.fold_in(seeds[8], part), 71), part)
    return {"hidden": hidden, "query_weight": query_weight, "adapter_shrink": adapter_shrink, "adapter_expand": adapter_expand, "adapter_page_table": adapter_page_table, "request_adapter_index": request_adapter_index, "key_value_cache": key_value_cache, "cached_lengths": cached_lengths}


def attend(queries, key_value_cache, cached_lengths):
    req_count = queries.shape[0]
    cache_len = key_value_cache.shape[1]
    queries = queries.astype(jnp.float32).reshape(req_count, KVH, QUERY_HEADS // KVH, HEAD_SIZE)
    key_rows = key_value_cache[:, :, 0, :].astype(jnp.float32).reshape(req_count, cache_len, KVH, HEAD_SIZE)
    values = key_value_cache[:, :, 1, :].astype(jnp.float32).reshape(req_count, cache_len, KVH, HEAD_SIZE)
    scores = jnp.einsum('tkgd,tckd->tkgc', queries, key_rows) * (1.0 / math.sqrt(HEAD_SIZE))
    in_range = jnp.arange(cache_len, dtype=jnp.int32)[None, :] < cached_lengths[:, None]
    scores = jnp.where(in_range[:, None, None, :], scores, -jnp.inf)
    largest = lax.optimization_barrier(jnp.max(scores, axis=-1, keepdims=True))
    powers = jnp.exp(scores - largest)
    weights = (powers / lax.optimization_barrier(jnp.sum(powers, axis=-1, keepdims=True))).astype(jnp.bfloat16)
    mixture = jnp.einsum('tkgc,tckd->tkgd', weights.astype(jnp.float32), values)
    return mixture.astype(jnp.bfloat16).reshape(req_count, QUERY_HEADS * HEAD_SIZE)

def reference(hidden, query_weight, adapter_shrink, adapter_expand, adapter_page_table, request_adapter_index, key_value_cache, cached_lengths):
    adapter_page = adapter_page_table[request_adapter_index].astype(jnp.int32)
    base_q = jnp.dot(hidden, query_weight, preferred_element_type=jnp.float32)
    block_count = REQS // 32

    def adapt(pieces):
        row_block, adapter_page_block = pieces
        shrink_weight_rows = adapter_shrink[adapter_page_block].astype(jnp.float32)
        reduced_features = jnp.einsum('td,tdr->tr', row_block.astype(jnp.float32), shrink_weight_rows).astype(jnp.bfloat16)
        expand_weight_rows = adapter_expand[adapter_page_block].astype(jnp.float32)
        return jnp.einsum('tr,trc->tc', reduced_features.astype(jnp.float32), expand_weight_rows)
    correction = lax.map(adapt, (hidden.reshape(block_count, 32, MODEL_WIDTH), adapter_page.reshape(block_count, 32)))
    queries = (base_q + correction.reshape(REQS, QUERY_HEADS * HEAD_SIZE)).astype(jnp.bfloat16)

    def attend_block(pieces):
        return attend(pieces[0], pieces[1], pieces[2])
    attended = lax.map(attend_block, (queries.reshape(block_count, 32, QUERY_HEADS * HEAD_SIZE), key_value_cache.reshape(block_count, 32, CACHE, 2, KVH * HEAD_SIZE), cached_lengths.reshape(block_count, 32)))
    return attended.reshape(REQS, QUERY_HEADS * HEAD_SIZE)
```

```python
import functools
import math

import jax
import jax.numpy as jnp
from jax import lax
from jax.experimental import pallas as pl
from jax.experimental.pallas import tpu as pltpu
from jax.sharding import PartitionSpec as P

QUERY_HEADS = 32
KVH = 4
HEAD_SIZE = 128
MESH = pl.DeviceIdType.MESH
F32 = jnp.float32
BF16 = jnp.bfloat16


def dot(a, b, dims=((1,), (0,)), precision=None):
    return lax.dot_general(a, b, (dims, ((), ())), preferred_element_type=F32, precision=precision)


def query_kernel(
    hidden, pages, weight, shrink, expand,
    out,
    xg, pg, wv, sv, ev, xsend, xrecv, part, parts, ret_send, ret_recv, qsend, base,
    w_sem, s_sem, e_sem, own_sem, pg_send, pg_recv, x_send, x_recv,
    d_send, d_recv, p_send, p_recv, r_send, r_recv, q_send, q_recv,
):
    nt, nd = lax.axis_size("tensor"), lax.axis_size("dp")
    t, g = lax.axis_index("tensor"), lax.axis_index("dp")
    own, width = hidden.shape
    rows = own * nt
    span = width // nt
    holders, rank = shrink.shape[0], shrink.shape[2]
    cols = weight.shape[1]
    slots = xsend.shape[0] // nd
    cap = 3 * rows // (2 * nd)
    cap = -(-cap // 8) * 8

    def tpeer(d):
        return lax.rem(t + d, nt)

    def dpeer(d):
        return lax.rem(g + d, nd)

    def mult(x, m):
        return pl.multiple_of(x * m, m)

    def w_copy(c):
        block = lax.rem(t + c, nt)
        return pltpu.make_async_copy(weight.at[pl.ds(mult(block, span), span), :], wv.at[c], w_sem.at[c])

    s_copy = pltpu.make_async_copy(shrink, sv, s_sem)
    e_copy = pltpu.make_async_copy(expand, ev, e_sem)
    w_copy(0).start()
    s_copy.start()
    for c in range(1, nt):
        w_copy(c).start()
    e_copy.start()

    ret_recv[...] = jnp.zeros_like(ret_recv)
    barrier = pltpu.get_barrier_semaphore()

    @pl.loop(1, nt)
    def _(d):
        pl.semaphore_signal(barrier, inc=1, device_id={"tensor": tpeer(d)}, device_id_type=MESH)

    @pl.loop(1, nd)
    def _(d):
        pl.semaphore_signal(barrier, inc=1, device_id={"dp": dpeer(d)}, device_id_type=MESH)

    pl.semaphore_wait(barrier, nt + nd - 2)

    my_rows = pl.ds(mult(t, own), own)

    def pg_copy(d):
        return pltpu.make_async_remote_copy(
            src_ref=pages, dst_ref=pg.at[my_rows, :], send_sem=pg_send.at[d], recv_sem=pg_recv.at[d],
            device_id={"tensor": tpeer(d)}, device_id_type=MESH)

    def x_copy(c, d):
        block = lax.rem(t + d + c, nt)
        return pltpu.make_async_remote_copy(
            src_ref=hidden.at[:, pl.ds(mult(block, span), span)], dst_ref=xg.at[c, my_rows, :],
            send_sem=x_send.at[c, d], recv_sem=x_recv.at[c, d],
            device_id={"tensor": tpeer(d)}, device_id_type=MESH)

    @pl.loop(1, nt)
    def _(d):
        pg_copy(d).start()
        x_copy(0, d).start()

    @pl.loop(1, nt)
    def _(c):
        @pl.loop(1, nt)
        def _(d):
            x_copy(c, d).start()

    def own_copy(c):
        block = lax.rem(t + c, nt)
        return pltpu.make_async_copy(
            hidden.at[:, pl.ds(mult(block, span), span)], xg.at[c, my_rows, :], own_sem.at[c])

    @pl.loop(0, nt)
    def _(c):
        own_copy(c).start()

    pg[my_rows, :] = pages[...]

    def wait_block(c):
        own_copy(c).wait()

        @pl.loop(1, nt)
        def _(d):
            x_copy(c, d).wait_recv()

    @pl.loop(1, nt)
    def _(d):
        pg_copy(d).wait_recv()

    page_all = pg[...]
    page_col = page_all[:, 0:1]
    lane = lax.broadcasted_iota(jnp.int32, (rows, 128), 1)
    hits = ((page_all >= lane * holders) & (page_all < (lane + 1) * holders)).astype(F32)
    lower = (lax.broadcasted_iota(jnp.int32, (rows, rows), 1)
             < lax.broadcasted_iota(jnp.int32, (rows, rows), 0)).astype(F32)
    before = dot(lower.astype(BF16), hits.astype(BF16))
    slot_of = jnp.sum(hits * (before + lane.astype(F32) * slots), axis=1, keepdims=True).astype(jnp.int32)
    place = (slot_of == lax.broadcasted_iota(jnp.int32, (rows, nd * slots), 1)).astype(F32).astype(BF16)
    page_bf = (page_all + 1).astype(F32).astype(BF16)

    wait_block(0)
    xsend[:, :span] = dot(place, xg[0], ((0,), (0,))).astype(BF16)
    xsend[:, span:] = dot(place, page_bf, ((0,), (0,))).astype(BF16)

    my_slots = pl.ds(mult(g, slots), slots)

    def d_copy(d):
        p = dpeer(d)
        return pltpu.make_async_remote_copy(
            src_ref=xsend.at[pl.ds(mult(p, slots), slots), :], dst_ref=xrecv.at[my_slots, :],
            send_sem=d_send.at[d], recv_sem=d_recv.at[d], device_id={"dp": p}, device_id_type=MESH)

    @pl.loop(1, nd)
    def _(d):
        d_copy(d).start()

    xrecv[my_slots, :] = xsend[my_slots, :]

    w_copy(0).wait()
    tile = min(cols, 256)

    def base_add(c, first):
        @pl.loop(0, cols // tile)
        def _(j):
            at = pl.ds(mult(j, tile), tile)
            term = dot(xg[c], wv[c, :, at])
            base[:, at] = term if first else base[:, at] + term

    base_add(0, True)
    s_copy.wait()

    @pl.loop(1, nd)
    def _(d):
        d_copy(d).wait_recv()

    resident = (xrecv[:, span:span + 128].astype(F32)).astype(jnp.int32)[:, 0:1] - 1 - g * holders
    part[...] = jnp.zeros_like(part)

    @pl.loop(0, holders)
    def _(o):
        y = dot(xrecv[:, :span], sv[o])
        part[:, :rank] = part[:, :rank] + jnp.where(resident == o, y, 0.0)

    def p_copy(d):
        return pltpu.make_async_remote_copy(
            src_ref=part, dst_ref=parts.at[t], send_sem=p_send.at[d], recv_sem=p_recv.at[d],
            device_id={"tensor": tpeer(d)}, device_id_type=MESH)

    @pl.loop(1, nt)
    def _(d):
        p_copy(d).start()

    parts[t] = part[...]

    @pl.loop(1, nt)
    def _(c):
        wait_block(c)
        w_copy(c).wait()
        base_add(c, False)

    e_copy.wait()

    @pl.loop(1, nt)
    def _(d):
        p_copy(d).wait_recv()

    total = parts[0]
    for i in range(1, nt):
        total = total + parts[i]
    reduced = total[:, :rank].astype(BF16).astype(F32)
    spread = jnp.concatenate(
        [jnp.where(resident == o, reduced, 0.0) for o in range(holders)], axis=1).astype(BF16)
    ret_send[...] = dot(spread, ev[...])

    def r_copy(d):
        p = dpeer(d)
        return pltpu.make_async_remote_copy(
            src_ref=ret_send.at[pl.ds(mult(p, slots), cap), :],
            dst_ref=ret_recv.at[pl.ds(mult(g, slots), cap), :],
            send_sem=r_send.at[d], recv_sem=r_recv.at[d], device_id={"dp": p}, device_id_type=MESH)

    @pl.loop(1, nd)
    def _(d):
        r_copy(d).start()

    ret_recv[my_slots, :] = ret_send[my_slots, :]

    @pl.loop(1, nd)
    def _(d):
        r_copy(d).wait_recv()

    high = ret_recv[...].astype(BF16)
    low = (ret_recv[...] - high.astype(F32)).astype(BF16)
    qsend[...] = (base[...] + (dot(place, high) + dot(place, low))).astype(BF16)

    def q_copy(d):
        p = tpeer(d)
        return pltpu.make_async_remote_copy(
            src_ref=qsend.at[pl.ds(mult(p, own), own), :], dst_ref=out.at[t],
            send_sem=q_send.at[d], recv_sem=q_recv.at[d],
            device_id={"tensor": p}, device_id_type=MESH)

    @pl.loop(1, nt)
    def _(d):
        q_copy(d).start()

    out[t] = qsend[my_rows, :]

    @pl.loop(1, nt)
    def _(d):
        q_copy(d).wait_recv()

    @pl.loop(1, nt)
    def _(d):
        pg_copy(d).wait_send()
        p_copy(d).wait_send()
        q_copy(d).wait_send()

        @pl.loop(0, nt)
        def _(c):
            x_copy(c, d).wait_send()

    @pl.loop(1, nd)
    def _(d):
        d_copy(d).wait_send()
        r_copy(d).wait_send()


def attend_kernel(lengths, queries, cache, out):
    step = pl.program_id(0)
    length = lengths[step]
    cache_len = cache.shape[1]
    keys = cache[0, :, 0, :]
    values = cache[0, :, 1, :]
    group = QUERY_HEADS // KVH
    in_range = lax.broadcasted_iota(jnp.int32, (group, cache_len), 1) < length
    for k in range(KVH):
        at = slice(k * HEAD_SIZE, (k + 1) * HEAD_SIZE)
        q = queries[0, k * group:(k + 1) * group, :]
        scores = dot(q, keys[:, at], ((1,), (1,))) * (1.0 / math.sqrt(HEAD_SIZE))
        scores = jnp.where(in_range, scores, -jnp.inf)
        powers = jnp.exp(scores - jnp.max(scores, axis=1, keepdims=True))
        weights = (powers / jnp.sum(powers, axis=1, keepdims=True)).astype(BF16)
        out[0, k * group:(k + 1) * group, :] = dot(weights, values[:, at]).astype(BF16)


def attend(queries, key_value_cache, cached_lengths):
    own, cache_len, _, kv_width = key_value_cache.shape
    return pl.pallas_call(
        attend_kernel,
        out_shape=jax.ShapeDtypeStruct((own, QUERY_HEADS, HEAD_SIZE), BF16),
        grid_spec=pltpu.PrefetchScalarGridSpec(
            num_scalar_prefetch=1,
            grid=(own,),
            in_specs=[
                pl.BlockSpec((1, QUERY_HEADS, HEAD_SIZE), lambda i, n: (i, 0, 0)),
                pl.BlockSpec((1, cache_len, 2, kv_width), lambda i, n: (i, 0, 0, 0)),
            ],
            out_specs=pl.BlockSpec((1, QUERY_HEADS, HEAD_SIZE), lambda i, n: (i, 0, 0)),
        ),
    )(cached_lengths, queries, key_value_cache)


def local(hidden, query_weight, adapter_shrink, adapter_expand, adapter_page_table,
          request_adapter_index, key_value_cache, cached_lengths):
    nt, nd = lax.axis_size("tensor"), lax.axis_size("dp")
    own, width = hidden.shape
    rows = own * nt
    span = width // nt
    holders, _, rank = adapter_shrink.shape
    cols = query_weight.shape[1]
    slots = -(-3 * rows // (2 * nd) // 16) * 16
    matches = request_adapter_index[:, None] == jnp.arange(adapter_page_table.shape[0], dtype=jnp.int32)[None, :]
    pages = jnp.sum(jnp.where(matches, adapter_page_table[None, :], 0), axis=1)
    pages = jnp.broadcast_to(pages[:, None], (own, 128))
    vmem = pl.BlockSpec(memory_space=pltpu.VMEM)
    hbm = pl.BlockSpec(memory_space=pl.ANY)
    dma = pltpu.SemaphoreType.DMA
    queries = pl.pallas_call(
        query_kernel,
        out_shape=jax.ShapeDtypeStruct((nt, own, cols), BF16),
        in_specs=[vmem, vmem, hbm, hbm, hbm],
        out_specs=vmem,
        scratch_shapes=[
            pltpu.VMEM((nt, rows, span), BF16),
            pltpu.VMEM((rows, 128), jnp.int32),
            pltpu.VMEM((nt, span, cols), BF16),
            pltpu.VMEM(adapter_shrink.shape, BF16),
            pltpu.VMEM((holders * rank, cols), BF16),
            pltpu.VMEM((nd * slots, span + 128), BF16),
            pltpu.VMEM((nd * slots, span + 128), BF16),
            pltpu.VMEM((nd * slots, 128), F32),
            pltpu.VMEM((nt, nd * slots, 128), F32),
            pltpu.VMEM((nd * slots, cols), F32),
            pltpu.VMEM((nd * slots, cols), F32),
            pltpu.VMEM((rows, cols), BF16),
            pltpu.VMEM((rows, cols), F32),
            dma((nt,)), dma, dma, dma((nt,)), dma((nt,)), dma((nt,)), dma((nt, nt)), dma((nt, nt)),
            dma((nd,)), dma((nd,)), dma((nt,)), dma((nt,)), dma((nd,)), dma((nd,)), dma((nt,)), dma((nt,)),
        ],
        compiler_params=pltpu.CompilerParams(
            collective_id=0, has_side_effects=True, vmem_limit_bytes=56 * 1024 * 1024),
    )(hidden, pages, query_weight, adapter_shrink, adapter_expand.reshape(holders * rank, cols))
    queries = queries.transpose(1, 0, 2).reshape(own, QUERY_HEADS, HEAD_SIZE)
    attended = attend(queries, key_value_cache, cached_lengths)
    return attended.reshape(own, QUERY_HEADS * HEAD_SIZE)


def solution(mesh):
    in_specs = (
        P(("groups", "dp", "tensor"), None),
        P(None, "tensor"),
        P("dp", "tensor", None),
        P("dp", None, "tensor"),
        P("groups"),
        P(("groups", "dp", "tensor")),
        P(("groups", "dp", "tensor"), None, None, None),
        P(("groups", "dp", "tensor")),
    )
    out_specs = P(("groups", "dp", "tensor"), None)
    return jax.shard_map(local, mesh=mesh, in_specs=in_specs, out_specs=out_specs, check_vma=False)
```

```python
import functools
import math

import jax
import jax.numpy as jnp
from jax import lax
from jax.experimental import pallas as pl
from jax.experimental.pallas import tpu as pltpu
from jax.sharding import PartitionSpec as P

QUERY_HEADS = 32
KVH = 4
HEAD_SIZE = 128
ADAPTER_RANK = 64
MESH = pl.DeviceIdType.MESH
F32 = jnp.float32
BF16 = jnp.bfloat16


def dot(a, b, dims=((1,), (0,)), precision=None):
    return lax.dot_general(a, b, (dims, ((), ())), preferred_element_type=F32, precision=precision)


def query_kernel(
    lengths, hidden, pages, weight, shrink, expand, cache,
    out,
    kv_in, kv, q_own, q_in, kv_sem,
    xg, pg, wv, sv, ev, xsend, xrecv, part, parts, ret_send, ret_recv, qsend, base,
    w_sem, s_sem, e_sem, own_sem, pg_send, pg_recv, x_send, x_recv,
    d_send, d_recv, p_send, p_recv, r_send, r_recv, q_send, q_recv,
):
    nt, nd = lax.axis_size("tensor"), lax.axis_size("dp")
    t, g = lax.axis_index("tensor"), lax.axis_index("dp")
    own, width = hidden.shape
    rows = own * nt
    span = width // nt
    rank = ADAPTER_RANK
    holders = shrink.shape[0] // rank
    cols = weight.shape[1]
    slots = xsend.shape[0] // nd
    cap = 3 * rows // (2 * nd)
    cap = -(-cap // 8) * 8

    def tpeer(d):
        return lax.rem(t + d, nt)

    def dpeer(d):
        return lax.rem(g + d, nd)

    def mult(x, m):
        return pl.multiple_of(x * m, m)

    def w_copy(c):
        block = lax.rem(t + c, nt)
        return pltpu.make_async_copy(weight.at[pl.ds(mult(block, span), span), :], wv.at[c], w_sem.at[c])

    s_copy = pltpu.make_async_copy(shrink, sv, s_sem)
    e_copy = pltpu.make_async_copy(expand, ev, e_sem)
    kv_copy = pltpu.make_async_copy(cache, kv_in, kv_sem)
    w_copy(0).start()
    s_copy.start()
    kv_copy.start()
    for c in range(1, nt):
        w_copy(c).start()
    e_copy.start()

    ret_recv[...] = jnp.zeros_like(ret_recv)
    barrier = pltpu.get_barrier_semaphore()

    @pl.loop(1, nt)
    def _(d):
        pl.semaphore_signal(barrier, inc=1, device_id={"tensor": tpeer(d)}, device_id_type=MESH)

    @pl.loop(1, nd)
    def _(d):
        pl.semaphore_signal(barrier, inc=1, device_id={"dp": dpeer(d)}, device_id_type=MESH)

    pl.semaphore_wait(barrier, nt + nd - 2)

    my_rows = pl.ds(mult(t, own), own)

    def pg_copy(d):
        return pltpu.make_async_remote_copy(
            src_ref=pages, dst_ref=pg.at[my_rows, :], send_sem=pg_send.at[d], recv_sem=pg_recv.at[d],
            device_id={"tensor": tpeer(d)}, device_id_type=MESH)

    def x_copy(c, d):
        block = lax.rem(t + d + c, nt)
        return pltpu.make_async_remote_copy(
            src_ref=hidden.at[:, pl.ds(mult(block, span), span)], dst_ref=xg.at[c, my_rows, :],
            send_sem=x_send.at[c, d], recv_sem=x_recv.at[c, d],
            device_id={"tensor": tpeer(d)}, device_id_type=MESH)

    @pl.loop(1, nt)
    def _(d):
        pg_copy(d).start()
        x_copy(0, d).start()

    @pl.loop(1, nt)
    def _(c):
        @pl.loop(1, nt)
        def _(d):
            x_copy(c, d).start()

    def own_copy(c):
        block = lax.rem(t + c, nt)
        return pltpu.make_async_copy(
            hidden.at[:, pl.ds(mult(block, span), span)], xg.at[c, my_rows, :], own_sem.at[c])

    @pl.loop(0, nt)
    def _(c):
        own_copy(c).start()

    pg[my_rows, :] = pages[...]

    def wait_block(c):
        own_copy(c).wait()

        @pl.loop(1, nt)
        def _(d):
            x_copy(c, d).wait_recv()

    @pl.loop(1, nt)
    def _(d):
        pg_copy(d).wait_recv()

    page_all = pg[...]
    page_col = page_all[:, 0:1]
    lane = lax.broadcasted_iota(jnp.int32, (rows, 128), 1)
    hits = ((page_all >= lane * holders) & (page_all < (lane + 1) * holders)).astype(F32)
    lower = (lax.broadcasted_iota(jnp.int32, (rows, rows), 1)
             < lax.broadcasted_iota(jnp.int32, (rows, rows), 0)).astype(F32)
    before = dot(lower.astype(BF16), hits.astype(BF16))
    slot_of = jnp.sum(hits * (before + lane.astype(F32) * slots), axis=1, keepdims=True).astype(jnp.int32)
    place = (slot_of == lax.broadcasted_iota(jnp.int32, (rows, nd * slots), 1)).astype(F32).astype(BF16)
    page_bf = (page_all + 1).astype(F32).astype(BF16)

    wait_block(0)
    xsend[:, :span] = dot(place, xg[0], ((0,), (0,))).astype(BF16)
    xsend[:, span:] = dot(place, page_bf, ((0,), (0,))).astype(BF16)

    my_slots = pl.ds(mult(g, slots), slots)

    def d_copy(d):
        p = dpeer(d)
        return pltpu.make_async_remote_copy(
            src_ref=xsend.at[pl.ds(mult(p, slots), slots), :], dst_ref=xrecv.at[my_slots, :],
            send_sem=d_send.at[d], recv_sem=d_recv.at[d], device_id={"dp": p}, device_id_type=MESH)

    @pl.loop(1, nd)
    def _(d):
        d_copy(d).start()

    xrecv[my_slots, :] = xsend[my_slots, :]

    kv_copy.wait()

    def merge(i):
        kv[i] = kv_in[i].reshape(kv.shape[1], kv.shape[2])

    pl.loop(0, own // 2)(merge)
    w_copy(0).wait()
    tile = min(cols, 256)

    def base_add(c, first):
        @pl.loop(0, cols // tile)
        def _(j):
            at = pl.ds(mult(j, tile), tile)
            term = dot(xg[c], wv[c, :, at])
            base[:, at] = term if first else base[:, at] + term

    base_add(0, True)
    s_copy.wait()

    @pl.loop(1, nd)
    def _(d):
        d_copy(d).wait_recv()

    resident = (xrecv[:, span:span + 128].astype(F32)).astype(jnp.int32)[:, 0:1] - 1 - g * holders
    shrunk = dot(xrecv[:, :span], sv[...], ((1,), (1,)))
    half = lax.broadcasted_iota(jnp.int32, (nd * slots, 2 * rank), 1) // rank
    acc = jnp.zeros((nd * slots, 2 * rank), F32)
    for o in range(0, holders, 2):
        acc = acc + jnp.where(resident == half + o, shrunk[:, o * rank:(o + 2) * rank], 0.0)
    part[...] = acc

    def p_copy(d):
        return pltpu.make_async_remote_copy(
            src_ref=part, dst_ref=parts.at[t], send_sem=p_send.at[d], recv_sem=p_recv.at[d],
            device_id={"tensor": tpeer(d)}, device_id_type=MESH)

    @pl.loop(1, nt)
    def _(d):
        p_copy(d).start()

    parts[t] = part[...]
    pl.loop(own // 2, own)(merge)

    @pl.loop(1, nt)
    def _(c):
        wait_block(c)
        w_copy(c).wait()
        base_add(c, False)

    e_copy.wait()

    @pl.loop(1, nt)
    def _(d):
        p_copy(d).wait_recv()

    total = parts[0]
    for i in range(1, nt):
        total = total + parts[i]
    reduced = (total[:, :rank] + total[:, rank:]).astype(BF16).astype(F32)
    spread = jnp.concatenate(
        [jnp.where(resident == o, reduced, 0.0) for o in range(holders)], axis=1).astype(BF16)
    ret_send[...] = dot(spread, ev[...])

    def r_copy(d):
        p = dpeer(d)
        return pltpu.make_async_remote_copy(
            src_ref=ret_send.at[pl.ds(mult(p, slots), cap), :],
            dst_ref=ret_recv.at[pl.ds(mult(g, slots), cap), :],
            send_sem=r_send.at[d], recv_sem=r_recv.at[d], device_id={"dp": p}, device_id_type=MESH)

    @pl.loop(1, nd)
    def _(d):
        r_copy(d).start()

    ret_recv[my_slots, :] = ret_send[my_slots, :]

    @pl.loop(1, nd)
    def _(d):
        r_copy(d).wait_recv()

    high = ret_recv[...].astype(BF16)
    low = (ret_recv[...] - high.astype(F32)).astype(BF16)
    qsend[...] = (base[...] + (dot(place, high) + dot(place, low))).astype(BF16)

    def q_copy(d):
        p = tpeer(d)
        return pltpu.make_async_remote_copy(
            src_ref=qsend.at[pl.ds(mult(p, own), own), :], dst_ref=q_in.at[t],
            send_sem=q_send.at[d], recv_sem=q_recv.at[d],
            device_id={"tensor": p}, device_id_type=MESH)

    @pl.loop(1, nt)
    def _(d):
        q_copy(d).start()

    q_in[t] = qsend[my_rows, :]

    @pl.loop(1, nt)
    def _(d):
        q_copy(d).wait_recv()

    heads = cols // HEAD_SIZE
    for i in range(nt):
        q_own[:, i * heads:(i + 1) * heads, :] = q_in[i].astype(F32).reshape(own, heads, HEAD_SIZE)

    group = QUERY_HEADS // KVH
    places, kv_width = kv.shape[1], kv.shape[2]
    same = (lax.broadcasted_iota(jnp.int32, (QUERY_HEADS, kv_width), 0) // group
            == lax.broadcasted_iota(jnp.int32, (QUERY_HEADS, kv_width), 1) // HEAD_SIZE)
    spot = lax.broadcasted_iota(jnp.int32, (QUERY_HEADS, places), 1)
    batch = 4

    @pl.loop(0, own // batch)
    def _(b):
        for j in range(batch):
            i = b * batch + j
            q = jnp.where(same, jnp.concatenate([q_own[i]] * KVH, axis=1), 0.0).astype(BF16)
            both = kv[i]
            scores = dot(q, both, ((1,), (1,))) * (1.0 / math.sqrt(HEAD_SIZE))
            scores = jnp.where((spot < 2 * lengths[i]) & (spot % 2 == 0), scores, -jnp.inf)
            powers = jnp.exp(scores - jnp.max(scores, axis=1, keepdims=True))
            weights = powers / jnp.sum(powers, axis=1, keepdims=True)
            mixed = jnp.where(same, dot(pltpu.roll(weights, 1, 1).astype(BF16), both), 0.0)
            mine = mixed[:, :HEAD_SIZE]
            for k in range(1, KVH):
                mine = mine + mixed[:, k * HEAD_SIZE:(k + 1) * HEAD_SIZE]
            out[i] = mine.astype(BF16)

    @pl.loop(1, nt)
    def _(d):
        pg_copy(d).wait_send()
        p_copy(d).wait_send()
        q_copy(d).wait_send()

        @pl.loop(0, nt)
        def _(c):
            x_copy(c, d).wait_send()

    @pl.loop(1, nd)
    def _(d):
        d_copy(d).wait_send()
        r_copy(d).wait_send()


def local(hidden, query_weight, adapter_shrink, adapter_expand, adapter_page_table,
          request_adapter_index, key_value_cache, cached_lengths):
    nt, nd = lax.axis_size("tensor"), lax.axis_size("dp")
    own, width = hidden.shape
    rows = own * nt
    span = width // nt
    holders, _, rank = adapter_shrink.shape
    cols = query_weight.shape[1]
    slots = -(-3 * rows // (2 * nd) // 16) * 16
    matches = request_adapter_index[:, None] == jnp.arange(adapter_page_table.shape[0], dtype=jnp.int32)[None, :]
    pages = jnp.sum(jnp.where(matches, adapter_page_table[None, :], 0), axis=1)
    pages = jnp.broadcast_to(pages[:, None], (own, 128))
    vmem = pl.BlockSpec(memory_space=pltpu.VMEM)
    hbm = pl.BlockSpec(memory_space=pl.ANY)
    dma = pltpu.SemaphoreType.DMA
    cache_len, kv_width = key_value_cache.shape[1], key_value_cache.shape[3]
    attended = pl.pallas_call(
        query_kernel,
        out_shape=jax.ShapeDtypeStruct((own, QUERY_HEADS, HEAD_SIZE), BF16),
        in_specs=[pl.BlockSpec(memory_space=pltpu.SMEM), vmem, vmem, hbm, hbm, hbm, hbm],
        out_specs=vmem,
        scratch_shapes=[
            pltpu.VMEM(key_value_cache.shape, BF16),
            pltpu.VMEM((own, 2 * cache_len, kv_width), BF16),
            pltpu.VMEM((own, QUERY_HEADS, HEAD_SIZE), F32),
            pltpu.VMEM((nt, own, cols), BF16),
            dma,
            pltpu.VMEM((nt, rows, span), BF16),
            pltpu.VMEM((rows, 128), jnp.int32),
            pltpu.VMEM((nt, span, cols), BF16),
            pltpu.VMEM((holders * rank, span), BF16),
            pltpu.VMEM((holders * rank, cols), BF16),
            pltpu.VMEM((nd * slots, span + 128), BF16),
            pltpu.VMEM((nd * slots, span + 128), BF16),
            pltpu.VMEM((nd * slots, 128), F32),
            pltpu.VMEM((nt, nd * slots, 128), F32),
            pltpu.VMEM((nd * slots, cols), F32),
            pltpu.VMEM((nd * slots, cols), F32),
            pltpu.VMEM((rows, cols), BF16),
            pltpu.VMEM((rows, cols), F32),
            dma((nt,)), dma, dma, dma((nt,)), dma((nt,)), dma((nt,)), dma((nt, nt)), dma((nt, nt)),
            dma((nd,)), dma((nd,)), dma((nt,)), dma((nt,)), dma((nd,)), dma((nd,)), dma((nt,)), dma((nt,)),
        ],
        compiler_params=pltpu.CompilerParams(
            collective_id=0, has_side_effects=True, vmem_limit_bytes=56 * 1024 * 1024),
    )(cached_lengths, hidden, pages, query_weight,
      jnp.swapaxes(adapter_shrink, 1, 2).reshape(holders * rank, span),
      adapter_expand.reshape(holders * rank, cols), key_value_cache)
    return attended.reshape(own, QUERY_HEADS * HEAD_SIZE)


def solution(mesh):
    in_specs = (
        P(("groups", "dp", "tensor"), None),
        P(None, "tensor"),
        P("dp", "tensor", None),
        P("dp", None, "tensor"),
        P("groups"),
        P(("groups", "dp", "tensor")),
        P(("groups", "dp", "tensor"), None, None, None),
        P(("groups", "dp", "tensor")),
    )
    out_specs = P(("groups", "dp", "tensor"), None)
    return jax.shard_map(local, mesh=mesh, in_specs=in_specs, out_specs=out_specs, check_vma=False)
```
